32 devices in a mesh: gz: 8 (over z, y), col: 4 (over x, core).
Axes of the slice: x: 2, y: 2, z: 4, core: 2. Of those that a mesh axis runs over, the one named last changes fastest.
Arguments:
- volume: bfloat16 [32, 64, 32, 256], P(None, 'gz', 'col'), may hold values from -6 to 6
- cotangent: bfloat16 [64, 32, 16, 128], P(None, 'gz', 'col'), may hold values from -6 to 6
- weight: bfloat16 [64, 864], P('col'), may hold values from -0.21875 to 0.21875
- bias: bfloat16 [64], P('col'), may hold values from -1 to 1
Outputs:
- input_grad: bfloat16 [32, 64, 32, 256], P(None, 'gz', 'col')
- filter_grad: float32 [64, 864], P('col')
- bias_grad: float32 [64], P('col')
The draws below stay inside these ranges and needn't reach their ends.
All inputs are finite; a program needn't handle non-finite values.
Results may differ from the reference program's by a relative error of at most 0.006.
Values may be sent and summed in bfloat16 or wider, within the bound.
A program may use at most 64 MiB of HBM per device.

```python
import math
import jax
import jax.numpy as jnp
from jax import lax

CIN = 32
COUT = 64
TAPS = 27
ZO_DEV = 4
XO = 128
ZOUT = 32
YOUT = 16
ZIN = 64
YIN = 32
XIN = 256
N_GZ = 8


def block_scale(own_key, dims, cuts, least, top_value):
    def one(dim, blocks):
        heights = jax.random.uniform(jax.random.fold_in(jax.random.fold_in(own_key, 6), dim), (blocks,), jnp.float32, least / len(cuts), top_value / len(cuts))
        return jnp.repeat(jnp.exp(heights), dims[dim] // blocks).reshape((-1,) + (1,) * (len(dims) - dim - 1))

    gain = one(*cuts[0])
    for cut in cuts[1:]:
        gain = gain * one(*cut)
    return gain


def centred(key, shape, spread, bound, shards=(), kind=jnp.bfloat16):
    values = jax.random.normal(key, shape, jnp.float32) * spread
    if len(shards) > 0:
        values = block_scale(key, shape, shards, -0.22, 0.18) * values
    return jnp.clip(values, min=-bound, max=bound).astype(kind)


def setup_inputs(seed: int = 0) -> dict:
    splits = jax.random.split(jax.random.key(seed), 5)
    volume = centred(splits[0], (CIN, ZIN, YIN, XIN), 1.0, 6.0, ((1, 8), (2, 4)))
    cotangent = centred(splits[1], (COUT, ZOUT, YOUT, XO), 1.0, 6.0, ((1, 8), (2, 4)))
    weight = centred(splits[2], (COUT, TAPS * CIN), (TAPS * CIN) ** -0.5, 0.21875, ((0, 4),))
    bias = jnp.clip(jax.random.uniform(splits[3], (COUT,), jnp.float32, -1.0, 1.0) * block_scale(splits[3], (COUT,), ((0, 4),), -0.4, 0.0), -1.0, 1.0).astype(jnp.bfloat16)
    return dict(volume=volume, cotangent=cotangent, weight=weight, bias=bias)


PARITY = (((1, 0),), ((0, 1), (2, 0)))

def slope(value):
    sigmoid_value = jax.nn.sigmoid(value)
    return sigmoid_value * (1.0 + value * (1.0 - sigmoid_value))

def columns(extended, planes, rows):
    even_cells = extended[..., 0::2]
    odd_cells = extended[..., 1::2]
    chosen = (jnp.roll(odd_cells, 1, axis=-1), even_cells, odd_cells)
    stacked = []
    for depth in range(3):
        for height in range(3):
            for across in range(3):
                stacked.append(chosen[across][:, depth:depth + 2 * planes - 1:2, height:height + 2 * rows - 1:2, :])
    stacked = jnp.stack(stacked)
    return stacked.reshape(-1, planes * rows * stacked.shape[-1])

def spread_back(source, weight, planes, rows):
    wide = source.shape[-1]
    channels = weight.shape[1] // 27
    rolled = jnp.roll(source, -1, axis=-1)
    result = jnp.zeros((channels, 2 * planes, 2 * rows, 2 * wide), jnp.float32)
    for parity_z in range(2):
        for parity_y in range(2):
            for parity_x in range(2):
                total = jnp.zeros((channels, planes * rows * wide), jnp.float32)
                for depth, shift_z in PARITY[parity_z]:
                    for height, shift_y in PARITY[parity_y]:
                        for across, shift_x in PARITY[parity_x]:
                            tap = 9 * depth + 3 * height + across
                            part = weight[:, tap * channels:(tap + 1) * channels]
                            anchor = rolled if shift_x == 1 else source
                            block = anchor[:, shift_z:shift_z + planes, shift_y:shift_y + rows, :].reshape(source.shape[0], -1)
                            total = total + jnp.dot(part.T, block, preferred_element_type=jnp.float32)
                result = result.at[:, parity_z::2, parity_y::2, parity_x::2].set(total.reshape(channels, planes, rows, wide))
    return result

def reference(volume, cotangent, weight, bias):
    channels = volume.shape[0]
    total_planes = volume.shape[1]
    total_rows = volume.shape[2]
    out_planes = total_planes // 2
    out_rows = total_rows // 2
    outputs = cotangent.shape[0]

    def forward_block(block):
        start = (2 * ZO_DEV * block - 1).astype(jnp.int32)
        picks = ((start + jnp.arange(2 * ZO_DEV + 1, dtype=jnp.int32)) % total_planes).astype(jnp.int32)
        slab = jnp.take(volume, picks, axis=1)
        slab = jnp.concatenate([slab[:, :, -1:], slab], axis=2)
        gathered = columns(slab, ZO_DEV, out_rows)
        preact = jnp.dot(weight, gathered, preferred_element_type=jnp.float32) + bias.astype(jnp.float32)[:, None]
        upstream = lax.dynamic_slice_in_dim(cotangent, (block * ZO_DEV).astype(jnp.int32), ZO_DEV, 1).reshape(outputs, -1)
        pre_grad = (upstream.astype(jnp.float32) * slope(preact)).astype(jnp.bfloat16)
        filter_part = lax.dot_general(pre_grad, gathered, (((1,), (1,)), ((), ())), preferred_element_type=jnp.float32)
        return (pre_grad.reshape(outputs, ZO_DEV, out_rows, -1), filter_part, lax.optimization_barrier(jnp.sum(pre_grad.astype(jnp.float32), axis=1)))
    blocks = jnp.arange(N_GZ, dtype=jnp.int32)
    grads, filter_parts, bias_parts = lax.map(forward_block, blocks)
    pre_grad = jnp.moveaxis(grads, 0, 1).reshape(outputs, out_planes, out_rows, -1)
    scale = 1.0 / math.sqrt(out_planes * out_rows * pre_grad.shape[-1])
    filter_grad = lax.optimization_barrier(jnp.sum(filter_parts, axis=0)) * scale
    bias_grad = lax.optimization_barrier(jnp.sum(bias_parts, axis=0)) * scale

    def backward_block(block):
        picks = ((block * ZO_DEV + jnp.arange(ZO_DEV + 1, dtype=jnp.int32)) % out_planes).astype(jnp.int32)
        source = jnp.take(pre_grad, picks, axis=1)
        source = jnp.concatenate([source, source[:, :, :1]], axis=2)
        return spread_back(source, weight, ZO_DEV, out_rows).astype(jnp.bfloat16)
    parts = lax.map(backward_block, blocks)
    input_grad = jnp.moveaxis(parts, 0, 1).reshape(channels, total_planes, total_rows, -1)
    return (input_grad, filter_grad, bias_grad)
```

```python
import functools
import math

import jax
import jax.numpy as jnp
from jax import lax
from jax.experimental import pallas as pl
from jax.experimental.pallas import tpu as pltpu
from jax.sharding import PartitionSpec as P

MESH = pl.DeviceIdType.MESH
F32 = jnp.float32
BF16 = jnp.bfloat16
TAP_OF = {(0, 0): 1, (1, 0): 2, (1, 1): 0}
LANES = 128


def one_hot(shape, chosen):
    row = lax.broadcasted_iota(jnp.int32, shape, 0)
    column = lax.broadcasted_iota(jnp.int32, shape, 1)
    return jnp.where(chosen(row, column), 1.0, 0.0).astype(BF16)


def matmul(a, b):
    return jnp.dot(a, b, preferred_element_type=F32)


def kernel(
    n_gz, n_col, scale,
    vol, cot, weight,
    igrad, fgrad,
    cells, gathered, full, deltas, rolled, upstream, flat, back, stack,
    split, merge, to_rows, from_rows, swap,
    terms, slots, part, pieces, result,
    w_send, w_recv, v_send, v_recv, p_send, p_recv,
    r_send, r_recv, s_send, s_recv, g_send, g_recv,
):
    channels, planes_in, rows_in, wide_in = vol.shape
    planes, rows = planes_in // 2, rows_in // 2
    outputs = cot.shape[0]
    own = weight.shape[0]
    taps_wide = weight.shape[1]
    owners = taps_wide // LANES
    gz = lax.axis_index("gz")
    col = lax.axis_index("col")
    gz_next, gz_back = lax.rem(gz + 1, n_gz), lax.rem(gz + n_gz - 1, n_gz)
    col_next, col_back = lax.rem(col + 1, n_col), lax.rem(col + n_col - 1, n_col)

    barrier = pltpu.get_barrier_semaphore()
    for d in range(1, n_col):
        pl.semaphore_signal(
            barrier, inc=1, device_id=(gz, lax.rem(col + d, n_col)), device_id_type=MESH
        )

    def greet(d, carry):
        pl.semaphore_signal(
            barrier, inc=1, device_id=(lax.rem(gz + d, n_gz), col), device_id_type=MESH
        )
        return carry

    lax.fori_loop(1, n_gz, greet, 0)
    for there in ((gz_next, col_next), (gz_back, col_back)):
        pl.semaphore_signal(barrier, inc=1, device_id=there, device_id_type=MESH)

    side = wide_in
    split[...] = one_hot(
        (side, 3 * LANES),
        lambda r, c: r
        == jnp.where(
            c < LANES, 2 * c, jnp.where(c < 2 * LANES, 2 * (c - LANES) + 1, (2 * (c - 2 * LANES) + side - 1) % side)
        ),
    )
    merge[...] = one_hot((side, side), lambda r, c: c == 2 * (r % LANES) + r // LANES)
    area = channels * rows_in
    to_rows[...] = one_hot((area, area), lambda r, c: c == (r % channels) * rows_in + r // channels)
    from_rows[...] = one_hot((area, area), lambda r, c: c == (r % rows_in) * channels + r // rows_in)
    blocks = planes * rows
    group = swap.shape[0] // blocks
    swap[...] = one_hot(swap.shape, lambda r, c: c == (r % group) * blocks + r // group)

    def take_plane(p, carry):
        plane = vol[:, p].astype(F32).reshape(area, wide_in).astype(BF16)
        apart = matmul(plane, split[...]).astype(BF16)
        apart = matmul(to_rows[...], apart).astype(BF16)
        for y in range(rows_in):
            for t in range(3):
                cells[t, p + 1, y + 1] = apart[
                    y * channels : (y + 1) * channels, t * LANES : (t + 1) * LANES
                ]
        return carry

    take_plane(planes_in - 1, 0)
    pl.semaphore_wait(barrier, (n_col - 1) + (n_gz - 1) + 2)

    def send(src, dst, send_sem, recv_sem, there):
        return pltpu.make_async_remote_copy(
            src_ref=src, dst_ref=dst, send_sem=send_sem, recv_sem=recv_sem,
            device_id=there, device_id_type=MESH,
        )

    plane_copy = send(
        cells.at[0:2, planes_in, 1 : rows_in + 1], cells.at[0:2, 0, 1 : rows_in + 1],
        v_send.at[0], v_recv.at[0], (gz_next, col),
    )
    corner_copy = send(
        cells.at[0:2, planes_in, rows_in], cells.at[0:2, 0, 0],
        v_send.at[1], v_recv.at[1], (gz_next, col_next),
    )
    plane_copy.start()
    corner_copy.start()
    own_rows = pl.ds(pl.multiple_of(col * own, own), own)
    weight_copies = [
        send(
            weight, full.at[own_rows], w_send.at[d - 1], w_recv.at[d - 1],
            (gz, lax.rem(col + d, n_col)),
        )
        for d in range(1, n_col)
    ]
    for copy in weight_copies:
        copy.start()
    full[own_rows] = weight[...]
    lax.fori_loop(0, planes_in - 1, take_plane, 0)
    row_copy = send(
        cells.at[0:2, 1 : planes_in + 1, rows_in], cells.at[0:2, 1 : planes_in + 1, 0],
        v_send.at[2], v_recv.at[2], (gz, col_next),
    )
    row_copy.start()

    for g in range(outputs // group):
        piece = cot[g * group : (g + 1) * group].astype(F32).reshape(group * blocks, LANES)
        piece = matmul(swap[...], piece.astype(BF16))
        for b in range(blocks):
            upstream[b, g * group : (g + 1) * group] = piece[b * group : (b + 1) * group]
    first = 27 * channels
    spare = (taps_wide - first, gathered.shape[1])
    gathered[first:, :] = one_hot(spare, lambda r, c: r == 0)

    for copy in weight_copies:
        copy.wait()
    turned = full[...].astype(F32).T
    empty = jnp.zeros((channels, outputs), F32)
    for pz in range(2):
        for py in range(2):
            for px in range(2):
                kind = 4 * pz + 2 * py + px
                for sz in range(2):
                    for sy in range(2):
                        pair = []
                        for sx in range(2):
                            joined = ((pz, sz), (py, sy), (px, sx))
                            if all(j in TAP_OF for j in joined):
                                dz, dy, dx = (TAP_OF[j] for j in joined)
                                tap = 9 * dz + 3 * dy + dx
                                pair.append(turned[tap * channels : (tap + 1) * channels])
                            else:
                                pair.append(empty)
                        start = 2 * outputs * (2 * sz + sy)
                        back[
                            kind * channels : (kind + 1) * channels, start : start + 2 * outputs
                        ] = jnp.concatenate(pair, axis=1).astype(BF16)

    plane_copy.wait()
    corner_copy.wait()
    row_copy.wait()

    def turn(x, shift):
        return pltpu.roll(x.astype(F32), shift, 1).astype(BF16)

    for y in range(rows_in + 1):
        cells[2, 0, y] = turn(cells[1, 0, y], 1)
    for p in range(1, planes_in + 1):
        cells[2, p, 0] = turn(cells[1, p, 0], 1)

    def forward(k, carry):
        width = rows * LANES
        lanes = pl.ds(pl.multiple_of(k * width, width), width)
        for dz in range(3):
            for dy in range(3):
                for dx, t in enumerate((2, 0, 1)):
                    tap = 9 * dz + 3 * dy + dx
                    for j in range(rows):
                        place = pl.ds(pl.multiple_of(k * width + j * LANES, LANES), LANES)
                        gathered[tap * channels : (tap + 1) * channels, place] = cells[
                            t, 2 * k + dz, 2 * j + dy
                        ]
        preact = matmul(full[...], gathered[:, lanes])
        for j in range(rows):
            value = preact[:, j * LANES : (j + 1) * LANES]
            s = jax.nn.sigmoid(value)
            delta = upstream[k * rows + j] * (s * (1.0 + value * (1.0 - s)))
            delta = delta.astype(BF16)
            place = pl.ds(pl.multiple_of(k * width + j * LANES, LANES), LANES)
            flat[:, place] = delta
            deltas[k, j] = delta
            rolled[k, j] = turn(delta, LANES - 1)
        return carry

    lax.fori_loop(0, planes, forward, 0)
    halo_copies = [
        send(
            deltas.at[0, 0:rows], deltas.at[planes, 0:rows],
            p_send.at[0], p_recv.at[0], (gz_back, col),
        ),
        send(
            deltas.at[0, 0], deltas.at[planes, rows],
            p_send.at[1], p_recv.at[1], (gz_back, col_back),
        ),
        send(
            deltas.at[0:planes, 0], deltas.at[0:planes, rows],
            p_send.at[2], p_recv.at[2], (gz, col_back),
        ),
    ]
    for copy in halo_copies:
        copy.start()

    sums = lax.dot_general(
        flat[...], gathered[...], (((1,), (1,)), ((), ())), preferred_element_type=F32
    )
    for c in range(n_col):
        for i in range(owners):
            terms[c, i] = sums[c * own : (c + 1) * own, i * LANES : (i + 1) * LANES]
    term_copies = []
    for d in range(1, n_col):
        there = lax.rem(col + d, n_col)
        term_copies.append(
            send(terms.at[there], slots.at[d - 1], r_send.at[d - 1], r_recv.at[d - 1], (gz, there))
        )
    for copy in term_copies:
        copy.start()

    for copy in halo_copies:
        copy.wait()
    for j in range(rows + 1):
        rolled[planes, j] = turn(deltas[planes, j], LANES - 1)
    for k in range(planes):
        rolled[k, rows] = turn(deltas[k, rows], LANES - 1)

    def backward(k, carry):
        for sz in range(2):
            for sy in range(2):
                for sx, source in enumerate((deltas, rolled)):
                    start = outputs * (4 * sz + 2 * sy + sx)
                    for j in range(rows):
                        stack[start : start + outputs, j * LANES : (j + 1) * LANES] = source[
                            k + sz, j + sy
                        ]
        found = matmul(back[...], stack[...]).astype(BF16)
        for pz in range(2):
            tall = []
            for y in range(rows_in):
                j, py = y // 2, y % 2
                kind = 4 * pz + 2 * py
                tall.append(
                    jnp.concatenate(
                        [
                            found[
                                (kind + px) * channels : (kind + px + 1) * channels,
                                j * LANES : (j + 1) * LANES,
                            ]
                            for px in range(2)
                        ],
                        axis=1,
                    )
                )
            tall = jnp.concatenate(tall, axis=0)
            tall = matmul(tall, merge[...]).astype(BF16)
            tall = matmul(from_rows[...], tall)
            igrad[:, 2 * k + pz] = tall.reshape(channels, rows_in, wide_in).astype(BF16)
        return carry

    half = planes // 2
    lax.fori_loop(0, half, backward, 0)

    for copy in term_copies:
        copy.wait()
    total = terms[col]
    for d in range(1, n_col):
        total = total + slots[d - 1]
    part[...] = total

    def piece_copy(d):
        there = lax.rem(gz + d, n_gz)
        safe = lax.rem(there, owners)
        return there, send(
            part.at[safe], pieces.at[d - 1], s_send.at[d - 1], s_recv.at[d - 1], (there, col)
        )

    def piece_start(d, carry):
        there, copy = piece_copy(d)

        @pl.when(there < owners)
        def _():
            copy.start()

        return carry

    lax.fori_loop(1, n_gz, piece_start, 0)
    lax.fori_loop(half, planes - 1, backward, 0)

    def piece_sent(d, carry):
        there, copy = piece_copy(d)

        @pl.when(there < owners)
        def _():
            copy.wait_send()

        return carry

    lax.fori_loop(1, n_gz, piece_sent, 0)
    mine = lax.rem(gz, owners)

    def result_copy(d):
        return send(
            result.at[mine], result.at[mine], g_send.at[d - 1], g_recv.at[mine],
            (lax.rem(gz + d, n_gz), col),
        )

    @pl.when(gz < owners)
    def _():
        def collect(d, value):
            piece_copy(d)[1].wait_recv()
            return value + pieces[d - 1]

        result[mine] = lax.fori_loop(1, n_gz, collect, part[mine]) * scale

        def result_start(d, carry):
            result_copy(d).start()
            return carry

        lax.fori_loop(1, n_gz, result_start, 0)

    backward(planes - 1, 0)

    @pl.when(gz < owners)
    def _():
        def result_sent(d, carry):
            result_copy(d).wait_send()
            return carry

        lax.fori_loop(1, n_gz, result_sent, 0)

    for i in range(owners):

        @pl.when(gz != i)
        def _():
            send(
                result.at[i], result.at[i], g_send.at[0], g_recv.at[i], (gz_next, col)
            ).wait_recv()

    for i in range(owners):
        fgrad[:, i * LANES : (i + 1) * LANES] = result[i]


def local(n_gz, n_col, volume, cotangent, weight, bias):
    channels, planes_in, rows_in, wide_in = volume.shape
    outputs, planes, rows, wide = cotangent.shape
    own = weight.shape[0]
    taps_wide = -(-(weight.shape[1] + 1) // LANES) * LANES
    owners = taps_wide // LANES
    scale = 1.0 / math.sqrt(planes * rows * wide * n_gz * n_col)
    filters = jnp.concatenate(
        [
            weight,
            bias[:, None],
            jnp.zeros((own, taps_wide - weight.shape[1] - 1), weight.dtype),
        ],
        axis=1,
    )
    blocks = planes * rows
    area = channels * rows_in
    cells_out = blocks * wide
    vmem = pl.BlockSpec(memory_space=pltpu.VMEM)
    dma = pltpu.SemaphoreType.DMA
    input_grad, sums = pl.pallas_call(
        functools.partial(kernel, n_gz, n_col, scale),
        out_shape=(
            jax.ShapeDtypeStruct(volume.shape, BF16),
            jax.ShapeDtypeStruct((own, taps_wide), F32),
        ),
        in_specs=[vmem] * 3,
        out_specs=(vmem, vmem),
        scratch_shapes=[
            pltpu.VMEM((3, planes_in + 1, rows_in + 1, channels, LANES), BF16),
            pltpu.VMEM((taps_wide, cells_out), BF16),
            pltpu.VMEM((outputs, taps_wide), BF16),
            pltpu.VMEM((planes + 1, rows + 1, outputs, LANES), BF16),
            pltpu.VMEM((planes + 1, rows + 1, outputs, LANES), BF16),
            pltpu.VMEM((blocks, outputs, LANES), F32),
            pltpu.VMEM((outputs, cells_out), BF16),
            pltpu.VMEM((8 * channels, 8 * outputs), BF16),
            pltpu.VMEM((8 * outputs, rows * LANES), BF16),
            pltpu.VMEM((wide_in, 3 * LANES), BF16),
            pltpu.VMEM((wide_in, wide_in), BF16),
            pltpu.VMEM((area, area), BF16),
            pltpu.VMEM((area, area), BF16),
            pltpu.VMEM((16 * blocks, 16 * blocks), BF16),
            pltpu.VMEM((n_col, owners, own, LANES), F32),
            pltpu.VMEM((n_col - 1, owners, own, LANES), F32),
            pltpu.VMEM((owners, own, LANES), F32),
            pltpu.VMEM((n_gz - 1, own, LANES), F32),
            pltpu.VMEM((owners, own, LANES), F32),
            dma((n_col - 1,)), dma((n_col - 1,)),
            dma((3,)), dma((3,)),
            dma((3,)), dma((3,)),
            dma((n_col - 1,)), dma((n_col - 1,)),
            dma((n_gz - 1,)), dma((n_gz - 1,)),
            dma((n_gz - 1,)), dma((owners,)),
        ],
        compiler_params=pltpu.CompilerParams(
            collective_id=0, has_side_effects=True, vmem_limit_bytes=40 * 1024 * 1024
        ),
    )(volume, cotangent.reshape(outputs, blocks, wide), filters)
    width = weight.shape[1]
    return input_grad, sums[:, :width], sums[:, width]


def solution(mesh):
    placed = (P(None, "gz", "col", None), P(None, "gz", "col", None), P("col", None), P("col"))
    return jax.shard_map(
        functools.partial(local, mesh.shape["gz"], mesh.shape["col"]),
        mesh=mesh,
        in_specs=placed,
        out_specs=(P(None, "gz", "col", None), P("col", None), P("col")),
        check_vma=False,
    )
```

```python
import functools
import math

import jax
import jax.numpy as jnp
from jax import lax
from jax.experimental import pallas as pl
from jax.experimental.pallas import tpu as pltpu
from jax.sharding import PartitionSpec as P

MESH = pl.DeviceIdType.MESH
F32 = jnp.float32
BF16 = jnp.bfloat16
TAP_OF = {(0, 0): 1, (1, 0): 2, (1, 1): 0}
LANES = 128


def one_hot(shape, chosen):
    row = lax.broadcasted_iota(jnp.int32, shape, 0)
    column = lax.broadcasted_iota(jnp.int32, shape, 1)
    return jnp.where(chosen(row, column), 1.0, 0.0).astype(BF16)


def around(size, body, value):
    if size > 16:
        return lax.fori_loop(1, size, body, value)
    for d in range(1, size):
        value = body(d, value)
    return value


def matmul(a, b):
    return jnp.dot(a, b, preferred_element_type=F32)


def kernel(
    n_gz, n_col, scale,
    volume, cotangent, weight_in, bias_in,
    igrad, fgrad, bgrad,
    vol, cot, weight_own, bias_own, weight,
    cells, gathered, full, deltas, rolled, upstream, flat, back, stack,
    split, merge, to_rows, from_rows, swap,
    terms, slots, part, pieces, result,
    load, w_send, w_recv, v_send, v_recv, p_send, p_recv,
    r_send, r_recv, s_send, s_recv, g_send, g_recv,
):
    channels, planes_in, rows_in, wide_in = vol.shape
    planes, rows = planes_in // 2, rows_in // 2
    outputs = cot.shape[0]
    own, taps_wide = weight.shape
    owners = taps_wide // LANES
    gz = lax.axis_index("gz")
    col = lax.axis_index("col")
    gz_next, gz_back = lax.rem(gz + 1, n_gz), lax.rem(gz + n_gz - 1, n_gz)
    col_next, col_back = lax.rem(col + 1, n_col), lax.rem(col + n_col - 1, n_col)

    loads = [pltpu.make_async_copy(weight_in, weight_own, load.at[planes_in])]
    loads.append(pltpu.make_async_copy(bias_in, bias_own, load.at[planes_in + 1]))
    loads.append(pltpu.make_async_copy(cotangent, cot, load.at[planes_in + 2]))

    def plane_load(p):
        return pltpu.make_async_copy(volume.at[:, p], vol.at[:, p], load.at[p])

    plane_load(planes_in - 1).start()
    for copy in loads:
        copy.start()
    for p in range(planes_in - 1):
        plane_load(p).start()
    barrier = pltpu.get_barrier_semaphore()
    for d in range(1, n_col):
        pl.semaphore_signal(
            barrier, inc=1, device_id=(gz, lax.rem(col + d, n_col)), device_id_type=MESH
        )

    def greet(d, carry):
        pl.semaphore_signal(
            barrier, inc=1, device_id=(lax.rem(gz + d, n_gz), col), device_id_type=MESH
        )
        return carry

    around(n_gz, greet, 0)
    for there in ((gz_next, col_next), (gz_back, col_back)):
        pl.semaphore_signal(barrier, inc=1, device_id=there, device_id_type=MESH)

    side = wide_in
    split[...] = one_hot(
        (side, side), lambda r, c: r == 2 * (c % LANES) + c // LANES
    )
    merge[...] = one_hot((side, side), lambda r, c: c == 2 * (r % LANES) + r // LANES)
    area = channels * rows_in
    to_rows[...] = one_hot((area, area), lambda r, c: c == (r % channels) * rows_in + r // channels)
    from_rows[...] = one_hot((area, area), lambda r, c: c == (r % rows_in) * channels + r // rows_in)
    blocks = planes * rows
    group = swap.shape[0] // blocks
    swap[...] = one_hot(swap.shape, lambda r, c: c == (r % group) * blocks + r // group)

    loads[0].wait()
    loads[1].wait()
    taps_own = weight_own.shape[1]
    tail = taps_wide - LANES
    square = (own, own)
    diagonal = lax.broadcasted_iota(jnp.int32, square, 0) == lax.broadcasted_iota(
        jnp.int32, square, 1
    )
    spread = jnp.broadcast_to(bias_own[...].astype(F32), square)
    column = jnp.sum(jnp.where(diagonal, spread, 0.0), axis=1, keepdims=True)
    spare_own = (own, taps_wide - taps_own)
    column = jnp.where(lax.broadcasted_iota(jnp.int32, spare_own, 1) == 0, column, 0.0)
    weight[:, :tail] = weight_own[:, :tail]
    weight[:, tail:] = jnp.concatenate(
        [weight_own[:, tail:].astype(F32), column], axis=1
    ).astype(BF16)

    def take_plane(p):
        plane_load(p).wait()
        plane = vol[:, p].astype(F32).reshape(area, wide_in).astype(BF16)
        plane = matmul(to_rows[...], plane).astype(BF16)
        apart = matmul(plane, split[...])
        parts = [apart[:, :LANES], apart[:, LANES:]]
        parts.append(pltpu.roll(parts[1], 1, 1))
        for t in range(3):
            narrow = parts[t].astype(BF16)
            for y in range(rows_in):
                cells[t, p + 1, y + 1] = narrow[y * channels : (y + 1) * channels]

    take_plane(planes_in - 1)
    pl.semaphore_wait(barrier, (n_col - 1) + (n_gz - 1) + 2)

    def send(src, dst, send_sem, recv_sem, there):
        return pltpu.make_async_remote_copy(
            src_ref=src, dst_ref=dst, send_sem=send_sem, recv_sem=recv_sem,
            device_id=there, device_id_type=MESH,
        )

    plane_copy = send(
        cells.at[0:2, planes_in, 1 : rows_in + 1], cells.at[0:2, 0, 1 : rows_in + 1],
        v_send.at[0], v_recv.at[0], (gz_next, col),
    )
    corner_copy = send(
        cells.at[0:2, planes_in, rows_in], cells.at[0:2, 0, 0],
        v_send.at[1], v_recv.at[1], (gz_next, col_next),
    )
    plane_copy.start()
    corner_copy.start()
    own_rows = pl.ds(pl.multiple_of(col * own, own), own)
    weight_copies = [
        send(
            weight, full.at[own_rows], w_send.at[d - 1], w_recv.at[d - 1],
            (gz, lax.rem(col + d, n_col)),
        )
        for d in range(1, n_col)
    ]
    for copy in weight_copies:
        copy.start()
    full[own_rows] = weight[...]
    for p in range(planes_in - 1):
        take_plane(p)
    row_copy = send(
        cells.at[0:2, 1 : planes_in + 1, rows_in], cells.at[0:2, 1 : planes_in + 1, 0],
        v_send.at[2], v_recv.at[2], (gz, col_next),
    )
    row_copy.start()

    loads[2].wait()
    for g in range(outputs // group):
        piece = cot[g * group : (g + 1) * group].astype(F32).reshape(group * blocks, LANES)
        piece = matmul(swap[...], piece.astype(BF16))
        for b in range(blocks):
            upstream[b, g * group : (g + 1) * group] = piece[b * group : (b + 1) * group]
    first = 27 * channels
    spare = (taps_wide - first, gathered.shape[1])
    gathered[first:, :] = one_hot(spare, lambda r, c: r == 0)

    for copy in weight_copies:
        copy.wait()
    turned = full[...].astype(F32).T
    empty = jnp.zeros((channels, outputs), F32)
    for pz in range(2):
        for py in range(2):
            for px in range(2):
                kind = 4 * pz + 2 * py + px
                for sz in range(2):
                    for sy in range(2):
                        pair = []
                        for sx in range(2):
                            joined = ((pz, sz), (py, sy), (px, sx))
                            if all(j in TAP_OF for j in joined):
                                dz, dy, dx = (TAP_OF[j] for j in joined)
                                tap = 9 * dz + 3 * dy + dx
                                pair.append(turned[tap * channels : (tap + 1) * channels])
                            else:
                                pair.append(empty)
                        start = 2 * outputs * (2 * sz + sy)
                        back[
                            kind * channels : (kind + 1) * channels, start : start + 2 * outputs
                        ] = jnp.concatenate(pair, axis=1).astype(BF16)

    def turn(x, shift):
        return pltpu.roll(x.astype(F32), shift, 1).astype(BF16)

    def forward(some, start):
        for place, (k, j) in enumerate(some):
            lanes = slice(start + place * LANES, start + (place + 1) * LANES)
            for dz in range(3):
                for dy in range(3):
                    for dx, t in enumerate((2, 0, 1)):
                        tap = 9 * dz + 3 * dy + dx
                        gathered[tap * channels : (tap + 1) * channels, lanes] = cells[
                            t, 2 * k + dz, 2 * j + dy
                        ]
        stop = start + len(some) * LANES
        preact = matmul(full[...], gathered[:, start:stop])
        for place, (k, j) in enumerate(some):
            value = preact[:, place * LANES : (place + 1) * LANES]
            s = jax.nn.sigmoid(value)
            delta = upstream[k * rows + j] * (s * (1.0 + value * (1.0 - s)))
            narrow = delta.astype(BF16)
            flat[:, start + place * LANES : start + (place + 1) * LANES] = narrow
            deltas[k, j] = narrow
            rolled[k, j] = turn(narrow, LANES - 1)
        return stop

    inside = [(k, j) for k in range(1, planes) for j in range(1, rows)]
    border = [(0, j) for j in range(rows)] + [(k, 0) for k in range(1, planes)]
    reached = forward(inside, 0)
    plane_copy.wait()
    corner_copy.wait()
    row_copy.wait()
    for y in range(rows_in + 1):
        cells[2, 0, y] = turn(cells[1, 0, y], 1)
    for p in range(1, planes_in + 1):
        cells[2, p, 0] = turn(cells[1, p, 0], 1)
    forward(border, reached)
    halo_copies = [
        send(
            deltas.at[0, 0:rows], deltas.at[planes, 0:rows],
            p_send.at[0], p_recv.at[0], (gz_back, col),
        ),
        send(
            deltas.at[0, 0], deltas.at[planes, rows],
            p_send.at[1], p_recv.at[1], (gz_back, col_back),
        ),
        send(
            deltas.at[0:planes, 0], deltas.at[0:planes, rows],
            p_send.at[2], p_recv.at[2], (gz, col_back),
        ),
    ]
    for copy in halo_copies:
        copy.start()

    sums = lax.dot_general(
        flat[...], gathered[...], (((1,), (1,)), ((), ())), preferred_element_type=F32
    )
    for c in range(n_col):
        for i in range(owners):
            terms[c, i] = sums[c * own : (c + 1) * own, i * LANES : (i + 1) * LANES]
    term_copies = []
    for d in range(1, n_col):
        there = lax.rem(col + d, n_col)
        term_copies.append(
            send(terms.at[there], slots.at[d - 1], r_send.at[d - 1], r_recv.at[d - 1], (gz, there))
        )
    for copy in term_copies:
        copy.start()

    for copy in halo_copies:
        copy.wait()
    for j in range(rows + 1):
        rolled[planes, j] = turn(deltas[planes, j], LANES - 1)
    for k in range(planes):
        rolled[k, rows] = turn(deltas[k, rows], LANES - 1)

    def backward(k):
        for sz in range(2):
            for sy in range(2):
                for sx, source in enumerate((deltas, rolled)):
                    start = outputs * (4 * sz + 2 * sy + sx)
                    for j in range(rows):
                        stack[k % 2, start : start + outputs, j * LANES : (j + 1) * LANES] = source[
                            k + sz, j + sy
                        ]
        found = matmul(back[...], stack[k % 2]).astype(BF16)
        for pz in range(2):
            tall = []
            for y in range(rows_in):
                j, py = y // 2, y % 2
                kind = 4 * pz + 2 * py
                tall.append(
                    jnp.concatenate(
                        [
                            found[
                                (kind + px) * channels : (kind + px + 1) * channels,
                                j * LANES : (j + 1) * LANES,
                            ]
                            for px in range(2)
                        ],
                        axis=1,
                    )
                )
            tall = jnp.concatenate(tall, axis=0)
            tall = matmul(tall, merge[...]).astype(BF16)
            tall = matmul(from_rows[...], tall)
            igrad[:, 2 * k + pz] = tall.reshape(channels, rows_in, wide_in).astype(BF16)

    backward(0)

    for copy in term_copies:
        copy.wait()
    total = terms[col]
    for d in range(1, n_col):
        total = total + slots[d - 1]
    part[...] = total

    def piece_copy(d):
        there = lax.rem(gz + d, n_gz)
        safe = lax.rem(there, owners)
        return there, send(
            part.at[safe], pieces.at[d - 1], s_send.at[d - 1], s_recv.at[d - 1], (there, col)
        )

    def piece_start(d, carry):
        there, copy = piece_copy(d)

        @pl.when(there < owners)
        def _():
            copy.start()

        return carry

    around(n_gz, piece_start, 0)
    for k in range(1, planes - 1):
        backward(k)

    def piece_sent(d, carry):
        there, copy = piece_copy(d)

        @pl.when(there < owners)
        def _():
            copy.wait_send()

        return carry

    around(n_gz, piece_sent, 0)
    mine = lax.rem(gz, owners)

    def result_copy(d):
        return send(
            result.at[mine], result.at[mine], g_send.at[d - 1], g_recv.at[mine],
            (lax.rem(gz + d, n_gz), col),
        )

    @pl.when(gz < owners)
    def _():
        def collect(d, value):
            piece_copy(d)[1].wait_recv()
            return value + pieces[d - 1]

        result[mine] = around(n_gz, collect, part[mine]) * scale

        def result_start(d, carry):
            result_copy(d).start()
            return carry

        around(n_gz, result_start, 0)

    backward(planes - 1)

    @pl.when(gz < owners)
    def _():
        def result_sent(d, carry):
            result_copy(d).wait_send()
            return carry

        around(n_gz, result_sent, 0)

    for i in range(owners):

        @pl.when(gz != i)
        def _():
            send(
                result.at[i], result.at[i], g_send.at[0], g_recv.at[i], (gz_next, col)
            ).wait_recv()

    for i in range(owners - 1):
        fgrad[:, i * LANES : (i + 1) * LANES] = result[i]
    last = result[owners - 1]
    fgrad[:, tail:] = last[:, : taps_own - tail]
    column = jnp.broadcast_to(last[:, taps_own - tail : taps_own - tail + 1], square)
    bgrad[...] = jnp.sum(jnp.where(diagonal, column, 0.0), axis=0, keepdims=True)


def local(n_gz, n_col, volume, cotangent, weight, bias):
    channels, planes_in, rows_in, wide_in = volume.shape
    outputs, planes, rows, wide = cotangent.shape
    own = weight.shape[0]
    taps_wide = -(-(weight.shape[1] + 1) // LANES) * LANES
    owners = taps_wide // LANES
    scale = 1.0 / math.sqrt(planes * rows * wide * n_gz * n_col)
    blocks = planes * rows
    area = channels * rows_in
    cells_out = blocks * wide
    vmem = pl.BlockSpec(memory_space=pltpu.VMEM)
    hbm = pl.BlockSpec(memory_space=pltpu.HBM)
    dma = pltpu.SemaphoreType.DMA
    input_grad, filter_grad, bias_grad = pl.pallas_call(
        functools.partial(kernel, n_gz, n_col, scale),
        out_shape=(
            jax.ShapeDtypeStruct(volume.shape, BF16),
            jax.ShapeDtypeStruct(weight.shape, F32),
            jax.ShapeDtypeStruct((1, own), F32),
        ),
        in_specs=[hbm] * 4,
        out_specs=(vmem,) * 3,
        scratch_shapes=[
            pltpu.VMEM(volume.shape, BF16),
            pltpu.VMEM((outputs, blocks, wide), BF16),
            pltpu.VMEM(weight.shape, BF16),
            pltpu.VMEM((1, own), BF16),
            pltpu.VMEM((own, taps_wide), BF16),
            pltpu.VMEM((3, planes_in + 1, rows_in + 1, channels, LANES), BF16),
            pltpu.VMEM((taps_wide, cells_out), BF16),
            pltpu.VMEM((outputs, taps_wide), BF16),
            pltpu.VMEM((planes + 1, rows + 1, outputs, LANES), BF16),
            pltpu.VMEM((planes + 1, rows + 1, outputs, LANES), BF16),
            pltpu.VMEM((blocks, outputs, LANES), F32),
            pltpu.VMEM((outputs, cells_out), BF16),
            pltpu.VMEM((8 * channels, 8 * outputs), BF16),
            pltpu.VMEM((2, 8 * outputs, rows * LANES), BF16),
            pltpu.VMEM((wide_in, wide_in), BF16),
            pltpu.VMEM((wide_in, wide_in), BF16),
            pltpu.VMEM((area, area), BF16),
            pltpu.VMEM((area, area), BF16),
            pltpu.VMEM((16 * blocks, 16 * blocks), BF16),
            pltpu.VMEM((n_col, owners, own, LANES), F32),
            pltpu.VMEM((n_col - 1, owners, own, LANES), F32),
            pltpu.VMEM((owners, own, LANES), F32),
            pltpu.VMEM((n_gz - 1, own, LANES), F32),
            pltpu.VMEM((owners, own, LANES), F32),
            dma((planes_in + 3,)),
            dma((n_col - 1,)), dma((n_col - 1,)),
            dma((3,)), dma((3,)),
            dma((3,)), dma((3,)),
            dma((n_col - 1,)), dma((n_col - 1,)),
            dma((n_gz - 1,)), dma((n_gz - 1,)),
            dma((n_gz - 1,)), dma((owners,)),
        ],
        compiler_params=pltpu.CompilerParams(
            collective_id=0, has_side_effects=True, vmem_limit_bytes=60 * 1024 * 1024
        ),
    )(volume, cotangent.reshape(outputs, blocks, wide), weight, bias[None, :])
    return input_grad, filter_grad, bias_grad.reshape(own)


def solution(mesh):
    placed = (P(None, "gz", "col", None), P(None, "gz", "col", None), P("col", None), P("col"))
    return jax.shard_map(
        functools.partial(local, mesh.shape["gz"], mesh.shape["col"]),
        mesh=mesh,
        in_specs=placed,
        out_specs=(P(None, "gz", "col", None), P("col", None), P("col")),
        check_vma=False,
    )
```

```python
import functools
import math

import jax
import jax.numpy as jnp
from jax import lax
from jax.experimental import pallas as pl
from jax.experimental.pallas import tpu as pltpu
from jax.sharding import PartitionSpec as P

MESH = pl.DeviceIdType.MESH
F32 = jnp.float32
BF16 = jnp.bfloat16
TAP_OF = {(0, 0): 1, (1, 0): 2, (1, 1): 0}
LANES = 128


def one_hot(shape, chosen):
    row = lax.broadcasted_iota(jnp.int32, shape, 0)
    column = lax.broadcasted_iota(jnp.int32, shape, 1)
    return jnp.where(chosen(row, column), 1.0, 0.0).astype(BF16)


def around(size, body, value):
    if size > 16:
        return lax.fori_loop(1, size, body, value)
    for d in range(1, size):
        value = body(d, value)
    return value


def matmul(a, b):
    return jnp.dot(a, b, preferred_element_type=F32)


def kernel(
    n_gz, n_col, scale,
    volume, cotangent, weight_in, bias_in,
    igrad, fgrad, bgrad,
    vol, cot, weight_own, bias_own, weight,
    edge, cells, gathered, full, deltas, rolled, upstream, flat, back, stack,
    split, merge, to_rows, from_rows, swap,
    terms, slots, part, pieces, result,
    load, w_send, w_recv, v_send, v_recv, p_send, p_recv,
    r_send, r_recv, s_send, s_recv, g_send, g_recv,
):
    channels, planes_in, rows_in, wide_in = vol.shape
    planes, rows = planes_in // 2, rows_in // 2
    outputs = cot.shape[0]
    own, taps_wide = weight.shape
    owners = taps_wide // LANES
    gz = lax.axis_index("gz")
    col = lax.axis_index("col")
    gz_next, gz_back = lax.rem(gz + 1, n_gz), lax.rem(gz + n_gz - 1, n_gz)
    col_next, col_back = lax.rem(col + 1, n_col), lax.rem(col + n_col - 1, n_col)

    loads = [pltpu.make_async_copy(weight_in, weight_own, load.at[planes_in])]
    loads.append(pltpu.make_async_copy(bias_in, bias_own, load.at[planes_in + 1]))
    loads.append(pltpu.make_async_copy(cotangent, cot, load.at[planes_in + 2]))

    def plane_load(p):
        return pltpu.make_async_copy(volume.at[:, p], vol.at[:, p], load.at[p])

    plane_load(planes_in - 1).start()
    for copy in loads:
        copy.start()
    for p in range(planes_in - 1):
        plane_load(p).start()
    barrier = pltpu.get_barrier_semaphore()
    for d in range(1, n_col):
        pl.semaphore_signal(
            barrier, inc=1, device_id=(gz, lax.rem(col + d, n_col)), device_id_type=MESH
        )

    def greet(d, carry):
        pl.semaphore_signal(
            barrier, inc=1, device_id=(lax.rem(gz + d, n_gz), col), device_id_type=MESH
        )
        return carry

    around(n_gz, greet, 0)
    for there in ((gz_next, col_next), (gz_back, col_back)):
        pl.semaphore_signal(barrier, inc=1, device_id=there, device_id_type=MESH)

    side = wide_in
    split[...] = one_hot(
        (side, side), lambda r, c: r == 2 * (c % LANES) + c // LANES
    )
    merge[...] = one_hot((side, side), lambda r, c: c == 2 * (r % LANES) + r // LANES)
    area = channels * rows_in
    to_rows[...] = one_hot((area, area), lambda r, c: c == (r % channels) * rows_in + r // channels)
    from_rows[...] = one_hot((area, area), lambda r, c: c == (r % rows_in) * channels + r // rows_in)
    blocks = planes * rows
    group = swap.shape[0] // blocks
    swap[...] = one_hot(swap.shape, lambda r, c: c == (r % group) * blocks + r // group)

    loads[0].wait()
    loads[1].wait()
    taps_own = weight_own.shape[1]
    tail = taps_wide - LANES
    square = (own, own)
    diagonal = lax.broadcasted_iota(jnp.int32, square, 0) == lax.broadcasted_iota(
        jnp.int32, square, 1
    )
    spread = jnp.broadcast_to(bias_own[...].astype(F32), square)
    column = jnp.sum(jnp.where(diagonal, spread, 0.0), axis=1, keepdims=True)
    spare_own = (own, taps_wide - taps_own)
    column = jnp.where(lax.broadcasted_iota(jnp.int32, spare_own, 1) == 0, column, 0.0)
    weight[:, :tail] = weight_own[:, :tail]
    weight[:, tail:] = jnp.concatenate(
        [weight_own[:, tail:].astype(F32), column], axis=1
    ).astype(BF16)

    def keep(apart, p, first_row, count):
        parts = [apart[:, :LANES], apart[:, LANES:]]
        parts.append(pltpu.roll(parts[1], 1, 1))
        for t in range(3):
            narrow = parts[t].astype(BF16)
            for y in range(count):
                cells[t, p, first_row + y] = narrow[y * channels : (y + 1) * channels]

    def take_plane(plane, p, count):
        plane = plane.astype(F32).reshape(area, wide_in).astype(BF16)
        plane = matmul(to_rows[...], plane).astype(BF16)
        keep(matmul(plane, split[...]), p, 1, count)

    ends = []
    for p in range(planes_in):
        plane_load(p).wait()
        ends.append(vol[:, p].astype(F32)[:, rows_in - 1, :].astype(BF16))
    ends = matmul(jnp.concatenate(ends, axis=0), split[...])
    for p in range(planes_in):
        keep(ends[p * channels : (p + 1) * channels], p + 1, rows_in, 1)
    pl.semaphore_wait(barrier, (n_col - 1) + (n_gz - 1) + 2)

    def send(src, dst, send_sem, recv_sem, there):
        return pltpu.make_async_remote_copy(
            src_ref=src, dst_ref=dst, send_sem=send_sem, recv_sem=recv_sem,
            device_id=there, device_id_type=MESH,
        )

    plane_copy = send(
        vol.at[:, planes_in - 1], edge,
        v_send.at[0], v_recv.at[0], (gz_next, col),
    )
    corner_copy = send(
        cells.at[0:2, planes_in, rows_in], cells.at[0:2, 0, 0],
        v_send.at[1], v_recv.at[1], (gz_next, col_next),
    )
    own_rows = pl.ds(pl.multiple_of(col * own, own), own)
    weight_copies = [
        send(
            weight, full.at[own_rows], w_send.at[d - 1], w_recv.at[d - 1],
            (gz, lax.rem(col + d, n_col)),
        )
        for d in range(1, n_col)
    ]
    row_copy = send(
        cells.at[0:2, 1 : planes_in + 1, rows_in], cells.at[0:2, 1 : planes_in + 1, 0],
        v_send.at[2], v_recv.at[2], (gz, col_next),
    )
    plane_copy.start()
    row_copy.start()
    for copy in weight_copies:
        copy.start()
    corner_copy.start()
    full[own_rows] = weight[...]
    for p in range(planes_in):
        take_plane(vol[:, p], p + 1, rows_in - 1)

    loads[2].wait()
    for g in range(outputs // group):
        piece = cot[g * group : (g + 1) * group].astype(F32).reshape(group * blocks, LANES)
        piece = matmul(swap[...], piece.astype(BF16))
        for b in range(blocks):
            upstream[b, g * group : (g + 1) * group] = piece[b * group : (b + 1) * group]
    first = 27 * channels
    spare = (taps_wide - first, gathered.shape[1])
    gathered[first:, :] = one_hot(spare, lambda r, c: r == 0)

    for copy in weight_copies:
        copy.wait()
    turned = full[...].astype(F32).T
    empty = jnp.zeros((channels, outputs), F32)
    for pz in range(2):
        for py in range(2):
            for px in range(2):
                kind = 4 * pz + 2 * py + px
                for sz in range(2):
                    for sy in range(2):
                        pair = []
                        for sx in range(2):
                            joined = ((pz, sz), (py, sy), (px, sx))
                            if all(j in TAP_OF for j in joined):
                                dz, dy, dx = (TAP_OF[j] for j in joined)
                                tap = 9 * dz + 3 * dy + dx
                                pair.append(turned[tap * channels : (tap + 1) * channels])
                            else:
                                pair.append(empty)
                        start = 2 * outputs * (2 * sz + sy)
                        back[
                            kind * channels : (kind + 1) * channels, start : start + 2 * outputs
                        ] = jnp.concatenate(pair, axis=1).astype(BF16)

    def turn(x, shift):
        return pltpu.roll(x.astype(F32), shift, 1).astype(BF16)

    def forward(some, start):
        for place, (k, j) in enumerate(some):
            lanes = slice(start + place * LANES, start + (place + 1) * LANES)
            for dz in range(3):
                for dy in range(3):
                    for dx, t in enumerate((2, 0, 1)):
                        tap = 9 * dz + 3 * dy + dx
                        gathered[tap * channels : (tap + 1) * channels, lanes] = cells[
                            t, 2 * k + dz, 2 * j + dy
                        ]
        stop = start + len(some) * LANES
        preact = matmul(full[...], gathered[:, start:stop])
        for place, (k, j) in enumerate(some):
            value = preact[:, place * LANES : (place + 1) * LANES]
            s = jax.nn.sigmoid(value)
            delta = upstream[k * rows + j] * (s * (1.0 + value * (1.0 - s)))
            narrow = delta.astype(BF16)
            flat[:, start + place * LANES : start + (place + 1) * LANES] = narrow
            deltas[k, j] = narrow
            rolled[k, j] = turn(narrow, LANES - 1)
        return stop

    inside = [(k, j) for k in range(1, planes) for j in range(1, rows)]
    border = [(0, j) for j in range(rows)] + [(k, 0) for k in range(1, planes)]
    reached = forward(inside, 0)
    plane_copy.wait()
    corner_copy.wait()
    row_copy.wait()
    take_plane(edge[...], 0, rows_in)
    cells[2, 0, 0] = turn(cells[1, 0, 0], 1)
    for p in range(1, planes_in + 1):
        cells[2, p, 0] = turn(cells[1, p, 0], 1)
    forward(border, reached)
    halo_copies = [
        send(
            deltas.at[0, 0:rows], deltas.at[planes, 0:rows],
            p_send.at[0], p_recv.at[0], (gz_back, col),
        ),
        send(
            deltas.at[0, 0], deltas.at[planes, rows],
            p_send.at[1], p_recv.at[1], (gz_back, col_back),
        ),
        send(
            deltas.at[0:planes, 0], deltas.at[0:planes, rows],
            p_send.at[2], p_recv.at[2], (gz, col_back),
        ),
    ]
    for copy in halo_copies:
        copy.start()

    sums = lax.dot_general(
        flat[...], gathered[...], (((1,), (1,)), ((), ())), preferred_element_type=F32
    )
    for c in range(n_col):
        for i in range(owners):
            terms[c, i] = sums[c * own : (c + 1) * own, i * LANES : (i + 1) * LANES]
    term_copies = []
    for d in range(1, n_col):
        there = lax.rem(col + d, n_col)
        term_copies.append(
            send(terms.at[there], slots.at[d - 1], r_send.at[d - 1], r_recv.at[d - 1], (gz, there))
        )
    for copy in term_copies:
        copy.start()

    def backward(k):
        for sz in range(2):
            for sy in range(2):
                for sx, source in enumerate((deltas, rolled)):
                    start = outputs * (4 * sz + 2 * sy + sx)
                    for j in range(rows):
                        stack[k % 2, start : start + outputs, j * LANES : (j + 1) * LANES] = source[
                            k + sz, j + sy
                        ]
        found = matmul(back[...], stack[k % 2]).astype(BF16)
        for pz in range(2):
            tall = []
            for y in range(rows_in):
                j, py = y // 2, y % 2
                kind = 4 * pz + 2 * py
                tall.append(
                    jnp.concatenate(
                        [
                            found[
                                (kind + px) * channels : (kind + px + 1) * channels,
                                j * LANES : (j + 1) * LANES,
                            ]
                            for px in range(2)
                        ],
                        axis=1,
                    )
                )
            tall = jnp.concatenate(tall, axis=0)
            tall = matmul(tall, merge[...]).astype(BF16)
            tall = matmul(from_rows[...], tall)
            igrad[:, 2 * k + pz] = tall.reshape(channels, rows_in, wide_in).astype(BF16)


    for copy in term_copies:
        copy.wait()
    total = terms[col]
    for d in range(1, n_col):
        total = total + slots[d - 1]
    part[...] = total

    def piece_copy(d):
        there = lax.rem(gz + d, n_gz)
        safe = lax.rem(there, owners)
        return there, send(
            part.at[safe], pieces.at[d - 1], s_send.at[d - 1], s_recv.at[d - 1], (there, col)
        )

    def piece_start(d, carry):
        there, copy = piece_copy(d)

        @pl.when(there < owners)
        def _():
            copy.start()

        return carry

    around(n_gz, piece_start, 0)
    for copy in halo_copies:
        copy.wait()
    for j in range(rows + 1):
        rolled[planes, j] = turn(deltas[planes, j], LANES - 1)
    for k in range(planes):
        rolled[k, rows] = turn(deltas[k, rows], LANES - 1)

    half = planes // 2
    for k in range(half):
        backward(k)

    def piece_sent(d, carry):
        there, copy = piece_copy(d)

        @pl.when(there < owners)
        def _():
            copy.wait_send()

        return carry

    around(n_gz, piece_sent, 0)
    mine = lax.rem(gz, owners)

    def result_copy(d):
        return send(
            result.at[mine], result.at[mine], g_send.at[d - 1], g_recv.at[mine],
            (lax.rem(gz + d, n_gz), col),
        )

    @pl.when(gz < owners)
    def _():
        def collect(d, value):
            piece_copy(d)[1].wait_recv()
            return value + pieces[d - 1]

        result[mine] = around(n_gz, collect, part[mine]) * scale

        def result_start(d, carry):
            result_copy(d).start()
            return carry

        around(n_gz, result_start, 0)

    for k in range(half, planes):
        backward(k)

    @pl.when(gz < owners)
    def _():
        def result_sent(d, carry):
            result_copy(d).wait_send()
            return carry

        around(n_gz, result_sent, 0)

    for i in range(owners):

        @pl.when(gz != i)
        def _():
            send(
                result.at[i], result.at[i], g_send.at[0], g_recv.at[i], (gz_next, col)
            ).wait_recv()

    for i in range(owners - 1):
        fgrad[:, i * LANES : (i + 1) * LANES] = result[i]
    last = result[owners - 1]
    fgrad[:, tail:] = last[:, : taps_own - tail]
    column = jnp.broadcast_to(last[:, taps_own - tail : taps_own - tail + 1], square)
    bgrad[...] = jnp.sum(jnp.where(diagonal, column, 0.0), axis=0, keepdims=True)


def local(n_gz, n_col, volume, cotangent, weight, bias):
    channels, planes_in, rows_in, wide_in = volume.shape
    outputs, planes, rows, wide = cotangent.shape
    own = weight.shape[0]
    taps_wide = -(-(weight.shape[1] + 1) // LANES) * LANES
    owners = taps_wide // LANES
    scale = 1.0 / math.sqrt(planes * rows * wide * n_gz * n_col)
    blocks = planes * rows
    area = channels * rows_in
    cells_out = blocks * wide
    vmem = pl.BlockSpec(memory_space=pltpu.VMEM)
    hbm = pl.BlockSpec(memory_space=pltpu.HBM)
    dma = pltpu.SemaphoreType.DMA
    input_grad, filter_grad, bias_grad = pl.pallas_call(
        functools.partial(kernel, n_gz, n_col, scale),
        out_shape=(
            jax.ShapeDtypeStruct(volume.shape, BF16),
            jax.ShapeDtypeStruct(weight.shape, F32),
            jax.ShapeDtypeStruct((1, own), F32),
        ),
        in_specs=[hbm] * 4,
        out_specs=(vmem,) * 3,
        scratch_shapes=[
            pltpu.VMEM(volume.shape, BF16),
            pltpu.VMEM((outputs, blocks, wide), BF16),
            pltpu.VMEM(weight.shape, BF16),
            pltpu.VMEM((1, own), BF16),
            pltpu.VMEM((own, taps_wide), BF16),
            pltpu.VMEM((channels, rows_in, wide_in), BF16),
            pltpu.VMEM((3, planes_in + 1, rows_in + 1, channels, LANES), BF16),
            pltpu.VMEM((taps_wide, cells_out), BF16),
            pltpu.VMEM((outputs, taps_wide), BF16),
            pltpu.VMEM((planes + 1, rows + 1, outputs, LANES), BF16),
            pltpu.VMEM((planes + 1, rows + 1, outputs, LANES), BF16),
            pltpu.VMEM((blocks, outputs, LANES), F32),
            pltpu.VMEM((outputs, cells_out), BF16),
            pltpu.VMEM((8 * channels, 8 * outputs), BF16),
            pltpu.VMEM((2, 8 * outputs, rows * LANES), BF16),
            pltpu.VMEM((wide_in, wide_in), BF16),
            pltpu.VMEM((wide_in, wide_in), BF16),
            pltpu.VMEM((area, area), BF16),
            pltpu.VMEM((area, area), BF16),
            pltpu.VMEM((16 * blocks, 16 * blocks), BF16),
            pltpu.VMEM((n_col, owners, own, LANES), F32),
            pltpu.VMEM((n_col - 1, owners, own, LANES), F32),
            pltpu.VMEM((owners, own, LANES), F32),
            pltpu.VMEM((n_gz - 1, own, LANES), F32),
            pltpu.VMEM((owners, own, LANES), F32),
            dma((planes_in + 3,)),
            dma((n_col - 1,)), dma((n_col - 1,)),
            dma((3,)), dma((3,)),
            dma((3,)), dma((3,)),
            dma((n_col - 1,)), dma((n_col - 1,)),
            dma((n_gz - 1,)), dma((n_gz - 1,)),
            dma((n_gz - 1,)), dma((owners,)),
        ],
        compiler_params=pltpu.CompilerParams(
            collective_id=0, has_side_effects=True, vmem_limit_bytes=40 * 1024 * 1024
        ),
    )(pltpu.with_memory_space_constraint(volume, pltpu.HBM), *(pltpu.with_memory_space_constraint(x, pltpu.HBM) for x in (cotangent.reshape(outputs, blocks, wide), weight, bias[None, :])))
    return input_grad, filter_grad, bias_grad.reshape(own)


def solution(mesh):
    placed = (P(None, "gz", "col", None), P(None, "gz", "col", None), P("col", None), P("col"))
    return jax.shard_map(
        functools.partial(local, mesh.shape["gz"], mesh.shape["col"]),
        mesh=mesh,
        in_specs=placed,
        out_specs=(P(None, "gz", "col", None), P("col", None), P("col")),
        check_vma=False,
    )
```

```python
import functools
import math

import jax
import jax.numpy as jnp
from jax import lax
from jax.experimental import pallas as pl
from jax.experimental.pallas import tpu as pltpu
from jax.sharding import PartitionSpec as P

MESH = pl.DeviceIdType.MESH
F32 = jnp.float32
BF16 = jnp.bfloat16
TAP_OF = {(0, 0): 1, (1, 0): 2, (1, 1): 0}
LANES = 128


def one_hot(shape, chosen):
    row = lax.broadcasted_iota(jnp.int32, shape, 0)
    column = lax.broadcasted_iota(jnp.int32, shape, 1)
    return jnp.where(chosen(row, column), 1.0, 0.0).astype(BF16)


def around(size, body, value):
    if size > 16:
        return lax.fori_loop(1, size, body, value)
    for d in range(1, size):
        value = body(d, value)
    return value


def matmul(a, b):
    return jnp.dot(a, b, preferred_element_type=F32)


def kernel(
    n_gz, n_col, scale,
    volume, cotangent, weight_in, bias_in,
    igrad, fgrad, bgrad,
    vol, cot, weight_own, bias_own, weight,
    edge, cells, gathered, full, deltas, rolled, upstream, flat, back, stack,
    split, merge, to_rows, from_rows, swap,
    terms, slots, part, pieces, result,
    load, w_send, w_recv, v_send, v_recv, p_send, p_recv,
    r_send, r_recv, s_send, s_recv, g_send, g_recv,
):
    channels, planes_in, rows_in, wide_in = vol.shape
    planes, rows = planes_in // 2, rows_in // 2
    outputs = cot.shape[0]
    own, taps_wide = weight.shape
    owners = taps_wide // LANES
    gz = lax.axis_index("gz")
    col = lax.axis_index("col")
    gz_next, gz_back = lax.rem(gz + 1, n_gz), lax.rem(gz + n_gz - 1, n_gz)
    col_next, col_back = lax.rem(col + 1, n_col), lax.rem(col + n_col - 1, n_col)

    loads = [pltpu.make_async_copy(weight_in, weight_own, load.at[planes_in])]
    loads.append(pltpu.make_async_copy(bias_in, bias_own, load.at[planes_in + 1]))
    loads.append(pltpu.make_async_copy(cotangent, cot, load.at[planes_in + 2]))

    def plane_load(p):
        return pltpu.make_async_copy(volume.at[:, p], vol.at[:, p], load.at[p])

    plane_load(planes_in - 1).start()
    for copy in loads:
        copy.start()
    for p in range(planes_in - 1):
        plane_load(p).start()
    barrier = pltpu.get_barrier_semaphore()
    for d in range(1, n_col):
        pl.semaphore_signal(
            barrier, inc=1, device_id=(gz, lax.rem(col + d, n_col)), device_id_type=MESH
        )

    def greet(d, carry):
        pl.semaphore_signal(
            barrier, inc=1, device_id=(lax.rem(gz + d, n_gz), col), device_id_type=MESH
        )
        return carry

    around(n_gz, greet, 0)
    for there in ((gz_next, col_next), (gz_back, col_back)):
        pl.semaphore_signal(barrier, inc=1, device_id=there, device_id_type=MESH)

    side = wide_in
    split[...] = one_hot(
        (side, side), lambda r, c: r == 2 * (c % LANES) + c // LANES
    )
    merge[...] = one_hot((side, side), lambda r, c: c == 2 * (r % LANES) + r // LANES)
    area = channels * rows_in
    to_rows[...] = one_hot((area, area), lambda r, c: c == (r % channels) * rows_in + r // channels)
    from_rows[...] = one_hot((area, area), lambda r, c: c == (r % rows_in) * channels + r // rows_in)
    blocks = planes * rows
    group = swap.shape[0] // blocks
    swap[...] = one_hot(swap.shape, lambda r, c: c == (r % group) * blocks + r // group)

    loads[0].wait()
    loads[1].wait()
    taps_own = weight_own.shape[1]
    tail = taps_wide - LANES
    square = (own, own)
    diagonal = lax.broadcasted_iota(jnp.int32, square, 0) == lax.broadcasted_iota(
        jnp.int32, square, 1
    )
    spread = jnp.broadcast_to(bias_own[...].astype(F32), square)
    column = jnp.sum(jnp.where(diagonal, spread, 0.0), axis=1, keepdims=True)
    spare_own = (own, taps_wide - taps_own)
    column = jnp.where(lax.broadcasted_iota(jnp.int32, spare_own, 1) == 0, column, 0.0)
    weight[:, :tail] = weight_own[:, :tail]
    weight[:, tail:] = jnp.concatenate(
        [weight_own[:, tail:].astype(F32), column], axis=1
    ).astype(BF16)

    def keep(apart, p, first_row, count):
        parts = [apart[:, :LANES], apart[:, LANES:]]
        parts.append(pltpu.roll(parts[1], 1, 1))
        for t in range(3):
            narrow = parts[t].astype(BF16)
            for y in range(count):
                cells[t, p, first_row + y] = narrow[y * channels : (y + 1) * channels]

    def take_plane(plane, p, count):
        plane = plane.astype(F32).reshape(area, wide_in).astype(BF16)
        plane = matmul(to_rows[...], plane).astype(BF16)
        keep(matmul(plane, split[...]), p, 1, count)

    ends = []
    for p in range(planes_in):
        plane_load(p).wait()
        ends.append(vol[:, p].astype(F32)[:, rows_in - 1, :].astype(BF16))
    ends = matmul(jnp.concatenate(ends, axis=0), split[...])
    for p in range(planes_in):
        keep(ends[p * channels : (p + 1) * channels], p + 1, rows_in, 1)
    pl.semaphore_wait(barrier, (n_col - 1) + (n_gz - 1) + 2)

    def send(src, dst, send_sem, recv_sem, there):
        return pltpu.make_async_remote_copy(
            src_ref=src, dst_ref=dst, send_sem=send_sem, recv_sem=recv_sem,
            device_id=there, device_id_type=MESH,
        )

    plane_copy = send(
        vol.at[:, planes_in - 1], edge,
        v_send.at[0], v_recv.at[0], (gz_next, col),
    )
    corner_copy = send(
        cells.at[0:2, planes_in, rows_in], cells.at[0:2, 0, 0],
        v_send.at[1], v_recv.at[1], (gz_next, col_next),
    )
    own_rows = pl.ds(pl.multiple_of(col * own, own), own)
    weight_copies = [
        send(
            weight, full.at[own_rows], w_send.at[d - 1], w_recv.at[d - 1],
            (gz, lax.rem(col + d, n_col)),
        )
        for d in range(1, n_col)
    ]
    row_copy = send(
        cells.at[0:2, 1 : planes_in + 1, rows_in], cells.at[0:2, 1 : planes_in + 1, 0],
        v_send.at[2], v_recv.at[2], (gz, col_next),
    )
    plane_copy.start()
    row_copy.start()
    for copy in weight_copies:
        copy.start()
    corner_copy.start()
    full[own_rows] = weight[...]
    for p in range(planes_in):
        take_plane(vol[:, p], p + 1, rows_in - 1)

    loads[2].wait()
    for g in range(outputs // group):
        piece = cot[g * group : (g + 1) * group].astype(F32).reshape(group * blocks, LANES)
        piece = matmul(swap[...], piece.astype(BF16))
        for b in range(blocks):
            upstream[b, g * group : (g + 1) * group] = piece[b * group : (b + 1) * group]
    first = 27 * channels
    spare = (taps_wide - first, gathered.shape[1])
    gathered[first:, :] = one_hot(spare, lambda r, c: r == 0)

    for copy in weight_copies:
        copy.wait()
    turned = full[...].astype(F32).T
    empty = jnp.zeros((channels, outputs), F32)
    for pz in range(2):
        for py in range(2):
            for px in range(2):
                kind = 4 * pz + 2 * py + px
                for sz in range(2):
                    for sy in range(2):
                        pair = []
                        for sx in range(2):
                            joined = ((pz, sz), (py, sy), (px, sx))
                            if all(j in TAP_OF for j in joined):
                                dz, dy, dx = (TAP_OF[j] for j in joined)
                                tap = 9 * dz + 3 * dy + dx
                                pair.append(turned[tap * channels : (tap + 1) * channels])
                            else:
                                pair.append(empty)
                        start = 2 * outputs * (2 * sz + sy)
                        back[
                            kind * channels : (kind + 1) * channels, start : start + 2 * outputs
                        ] = jnp.concatenate(pair, axis=1).astype(BF16)

    def turn(x, shift):
        return pltpu.roll(x.astype(F32), shift, 1).astype(BF16)

    def forward(some, start):
        for place, (k, j) in enumerate(some):
            lanes = slice(start + place * LANES, start + (place + 1) * LANES)
            for dz in range(3):
                for dy in range(3):
                    for dx, t in enumerate((2, 0, 1)):
                        tap = 9 * dz + 3 * dy + dx
                        gathered[tap * channels : (tap + 1) * channels, lanes] = cells[
                            t, 2 * k + dz, 2 * j + dy
                        ]
        stop = start + len(some) * LANES
        preact = matmul(full[...], gathered[:, start:stop])
        for place, (k, j) in enumerate(some):
            value = preact[:, place * LANES : (place + 1) * LANES]
            s = jax.nn.sigmoid(value)
            delta = upstream[k * rows + j] * (s * (1.0 + value * (1.0 - s)))
            narrow = delta.astype(BF16)
            flat[:, start + place * LANES : start + (place + 1) * LANES] = narrow
            deltas[k, j] = narrow
        return stop

    inside = [(k, j) for k in range(1, planes) for j in range(1, rows)]
    border = [(0, j) for j in range(rows)] + [(k, 0) for k in range(1, planes)]
    reached = forward(inside, 0)
    row_copy.wait()
    for p in range(1, planes_in + 1):
        cells[2, p, 0] = turn(cells[1, p, 0], 1)
    plane_copy.wait()
    corner_copy.wait()
    take_plane(edge[...], 0, rows_in)
    cells[2, 0, 0] = turn(cells[1, 0, 0], 1)
    forward(border, reached)
    halo_copies = [
        send(
            deltas.at[0, 0:rows], deltas.at[planes, 0:rows],
            p_send.at[0], p_recv.at[0], (gz_back, col),
        ),
        send(
            deltas.at[0, 0], deltas.at[planes, rows],
            p_send.at[1], p_recv.at[1], (gz_back, col_back),
        ),
        send(
            deltas.at[0:planes, 0], deltas.at[0:planes, rows],
            p_send.at[2], p_recv.at[2], (gz, col_back),
        ),
    ]
    for copy in halo_copies:
        copy.start()

    sums = lax.dot_general(
        flat[...], gathered[...], (((1,), (1,)), ((), ())), preferred_element_type=F32
    )
    for c in range(n_col):
        for i in range(owners):
            terms[c, i] = sums[c * own : (c + 1) * own, i * LANES : (i + 1) * LANES]
    term_copies = []
    for d in range(1, n_col):
        there = lax.rem(col + d, n_col)
        term_copies.append(
            send(terms.at[there], slots.at[d - 1], r_send.at[d - 1], r_recv.at[d - 1], (gz, there))
        )
    for copy in term_copies:
        copy.start()
    for k in range(planes):
        for j in range(rows):
            rolled[k, j] = turn(deltas[k, j], LANES - 1)

    def backward(k):
        for sz in range(2):
            for sy in range(2):
                for sx, source in enumerate((deltas, rolled)):
                    start = outputs * (4 * sz + 2 * sy + sx)
                    for j in range(rows):
                        stack[k % 2, start : start + outputs, j * LANES : (j + 1) * LANES] = source[
                            k + sz, j + sy
                        ]
        found = matmul(back[...], stack[k % 2]).astype(BF16)
        for pz in range(2):
            tall = []
            for y in range(rows_in):
                j, py = y // 2, y % 2
                kind = 4 * pz + 2 * py
                tall.append(
                    jnp.concatenate(
                        [
                            found[
                                (kind + px) * channels : (kind + px + 1) * channels,
                                j * LANES : (j + 1) * LANES,
                            ]
                            for px in range(2)
                        ],
                        axis=1,
                    )
                )
            tall = jnp.concatenate(tall, axis=0)
            tall = matmul(tall, merge[...]).astype(BF16)
            tall = matmul(from_rows[...], tall)
            igrad[:, 2 * k + pz] = tall.reshape(channels, rows_in, wide_in).astype(BF16)


    for copy in term_copies:
        copy.wait()
    total = terms[col]
    for d in range(1, n_col):
        total = total + slots[d - 1]
    part[...] = total

    def piece_copy(d):
        there = lax.rem(gz + d, n_gz)
        safe = lax.rem(there, owners)
        return there, send(
            part.at[safe], pieces.at[d - 1], s_send.at[d - 1], s_recv.at[d - 1], (there, col)
        )

    def piece_start(d, carry):
        there, copy = piece_copy(d)

        @pl.when(there < owners)
        def _():
            copy.start()

        return carry

    around(n_gz, piece_start, 0)
    for copy in halo_copies:
        copy.wait()
    for j in range(rows + 1):
        rolled[planes, j] = turn(deltas[planes, j], LANES - 1)
    for k in range(planes):
        rolled[k, rows] = turn(deltas[k, rows], LANES - 1)

    half = planes // 2
    for k in range(half):
        backward(k)

    def piece_sent(d, carry):
        there, copy = piece_copy(d)

        @pl.when(there < owners)
        def _():
            copy.wait_send()

        return carry

    around(n_gz, piece_sent, 0)
    mine = lax.rem(gz, owners)

    def result_copy(d):
        return send(
            result.at[mine], result.at[mine], g_send.at[d - 1], g_recv.at[mine],
            (lax.rem(gz + d, n_gz), col),
        )

    @pl.when(gz < owners)
    def _():
        def collect(d, value):
            piece_copy(d)[1].wait_recv()
            return value + pieces[d - 1]

        result[mine] = around(n_gz, collect, part[mine]) * scale

        def result_start(d, carry):
            result_copy(d).start()
            return carry

        around(n_gz, result_start, 0)

    for k in range(half, planes):
        backward(k)

    @pl.when(gz < owners)
    def _():
        def result_sent(d, carry):
            result_copy(d).wait_send()
            return carry

        around(n_gz, result_sent, 0)

    for i in range(owners):

        @pl.when(gz != i)
        def _():
            send(
                result.at[i], result.at[i], g_send.at[0], g_recv.at[i], (gz_next, col)
            ).wait_recv()

    for i in range(owners - 1):
        fgrad[:, i * LANES : (i + 1) * LANES] = result[i]
    last = result[owners - 1]
    fgrad[:, tail:] = last[:, : taps_own - tail]
    column = jnp.broadcast_to(last[:, taps_own - tail : taps_own - tail + 1], square)
    bgrad[...] = jnp.sum(jnp.where(diagonal, column, 0.0), axis=0, keepdims=True)


def local(n_gz, n_col, volume, cotangent, weight, bias):
    channels, planes_in, rows_in, wide_in = volume.shape
    outputs, planes, rows, wide = cotangent.shape
    own = weight.shape[0]
    taps_wide = -(-(weight.shape[1] + 1) // LANES) * LANES
    owners = taps_wide // LANES
    scale = 1.0 / math.sqrt(planes * rows * wide * n_gz * n_col)
    blocks = planes * rows
    area = channels * rows_in
    cells_out = blocks * wide
    vmem = pl.BlockSpec(memory_space=pltpu.VMEM)
    hbm = pl.BlockSpec(memory_space=pltpu.HBM)
    dma = pltpu.SemaphoreType.DMA
    input_grad, filter_grad, bias_grad = pl.pallas_call(
        functools.partial(kernel, n_gz, n_col, scale),
        out_shape=(
            jax.ShapeDtypeStruct(volume.shape, BF16),
            jax.ShapeDtypeStruct(weight.shape, F32),
            jax.ShapeDtypeStruct((1, own), F32),
        ),
        in_specs=[hbm] * 4,
        out_specs=(vmem,) * 3,
        scratch_shapes=[
            pltpu.VMEM(volume.shape, BF16),
            pltpu.VMEM((outputs, blocks, wide), BF16),
            pltpu.VMEM(weight.shape, BF16),
            pltpu.VMEM((1, own), BF16),
            pltpu.VMEM((own, taps_wide), BF16),
            pltpu.VMEM((channels, rows_in, wide_in), BF16),
            pltpu.VMEM((3, planes_in + 1, rows_in + 1, channels, LANES), BF16),
            pltpu.VMEM((taps_wide, cells_out), BF16),
            pltpu.VMEM((outputs, taps_wide), BF16),
            pltpu.VMEM((planes + 1, rows + 1, outputs, LANES), BF16),
            pltpu.VMEM((planes + 1, rows + 1, outputs, LANES), BF16),
            pltpu.VMEM((blocks, outputs, LANES), F32),
            pltpu.VMEM((outputs, cells_out), BF16),
            pltpu.VMEM((8 * channels, 8 * outputs), BF16),
            pltpu.VMEM((2, 8 * outputs, rows * LANES), BF16),
            pltpu.VMEM((wide_in, wide_in), BF16),
            pltpu.VMEM((wide_in, wide_in), BF16),
            pltpu.VMEM((area, area), BF16),
            pltpu.VMEM((area, area), BF16),
            pltpu.VMEM((16 * blocks, 16 * blocks), BF16),
            pltpu.VMEM((n_col, owners, own, LANES), F32),
            pltpu.VMEM((n_col - 1, owners, own, LANES), F32),
            pltpu.VMEM((owners, own, LANES), F32),
            pltpu.VMEM((n_gz - 1, own, LANES), F32),
            pltpu.VMEM((owners, own, LANES), F32),
            dma((planes_in + 3,)),
            dma((n_col - 1,)), dma((n_col - 1,)),
            dma((3,)), dma((3,)),
            dma((3,)), dma((3,)),
            dma((n_col - 1,)), dma((n_col - 1,)),
            dma((n_gz - 1,)), dma((n_gz - 1,)),
            dma((n_gz - 1,)), dma((owners,)),
        ],
        compiler_params=pltpu.CompilerParams(
            collective_id=0, has_side_effects=True, vmem_limit_bytes=40 * 1024 * 1024
        ),
    )(pltpu.with_memory_space_constraint(volume, pltpu.HBM), *(pltpu.with_memory_space_constraint(x, pltpu.HBM) for x in (cotangent.reshape(outputs, blocks, wide), weight, bias[None, :])))
    return input_grad, filter_grad, bias_grad.reshape(own)


def solution(mesh):
    placed = (P(None, "gz", "col", None), P(None, "gz", "col", None), P("col", None), P("col"))
    return jax.shard_map(
        functools.partial(local, mesh.shape["gz"], mesh.shape["col"]),
        mesh=mesh,
        in_specs=placed,
        out_specs=(P(None, "gz", "col", None), P("col", None), P("col")),
        check_vma=False,
    )
```
